32 devices in a mesh: seq: 8 (over y, x, core), exp: 4 (over z).
Axes of the slice: x: 2, y: 2, z: 4, core: 2. Of those that a mesh axis runs over, the one named last changes fastest.
Arguments:
- hidden: bfloat16 [1024, 4096], P('seq', 'exp'), may hold values from -6 to 6
- queries: bfloat16 [1024, 4096], P('seq', 'exp'), may hold values from -40 to 40
- keys: bfloat16 [1024, 1024], P('seq', 'exp'), may hold values from -6 to 6
- values: bfloat16 [1024, 1024], P('seq', 'exp'), may hold values from -6 to 6
- block_place: int32 [16], replicated, may hold values from 0 to 15, as said below
- page_table: int32 [64], replicated, may hold values from 0 to 63, each once
- out_weight: bfloat16 [4096, 4096], P('exp'), may hold values from -0.09375 to 0.09375
- norm_gain: float32 [4096], replicated, may hold values from 0.5 to 2
- gate_probs: float32 [1024, 2], P('seq'), may hold values from 0.1 to 1
- routes: int32 [1024, 2], P('seq'), may hold values from 0 to 7, all different within a row; in each aligned block of 128 rows (0 to 127, 128 to 255, ...) at most 64 rows name the same one
- w_gate: bfloat16 [8, 4096, 14336], P('exp', None, 'seq'), may hold values from -0.09375 to 0.09375
- w_up: bfloat16 [8, 4096, 14336], P('exp', None, 'seq'), may hold values from -0.09375 to 0.09375
- w_down: bfloat16 [8, 14336, 4096], P('exp', 'seq'), may hold values from -0.046875 to 0.046875
Outputs:
- layer_out: bfloat16 [1024, 4096], P('seq', 'exp')
- key_value_pages: bfloat16 [64, 16, 2, 1024], P('seq', None, None, 'exp')
The draws below stay inside these ranges and needn't reach their ends.
Inputs may be any that keep to these rules, and one draw needn't show every extreme that they name: `block_place`: the first 12 entries are a permutation of 0 to 11, the others a permutation of 12 to 15. `page_table`: A permutation of the pages. `routes`: in the rows of one index of seq (128 rows) no expert is named more than 64 times, a bound that some block reaches; a row names two different experts.
All inputs are finite; a program needn't handle non-finite values.
Results may differ from the reference program's by a relative error of at most 0.02.
Values may be sent and summed in bfloat16 or wider, within the bound.
A program may use at most 192 MiB of HBM per device.

```python
import math
import jax
import jax.numpy as jnp
import numpy as np
from jax import lax

D = 4096
QUERY_HEADS = 32
KEY_VALUE_HEADS = 8
HEAD_SIZE = 128
NEXP = 8
TOP = 2
FF = 14336
TOKENS_PER_SEQ = 128
PAGE_TOKENS = 16
HALF = 64
CAP = 64
PROMPT_TOKENS = 1024
LONG = 768
BLOCKS = 16
LONG_BLOCKS = 12
PAGE_TOTAL = 64


def key_region(key):
    random_subkey = jax.random.fold_in(key, 11)
    return jnp.clip(jax.random.normal(random_subkey, (PROMPT_TOKENS, KEY_VALUE_HEADS * HEAD_SIZE), jnp.float32), -6.0, 6.0)


def draw_keys(key, part):
    return key_region(key).astype(jnp.bfloat16)


def draw_queries(key, part):
    base_field = jnp.clip(jax.random.normal(jax.random.fold_in(key, 23), (PROMPT_TOKENS, QUERY_HEADS * HEAD_SIZE), jnp.float32), -6.0, 6.0)
    return base_field.astype(jnp.bfloat16)


def draw_block_place(key, part):
    long_order = jax.random.permutation(jax.random.fold_in(key, 31), LONG_BLOCKS).astype(jnp.int32)
    short_order = jax.random.permutation(jax.random.fold_in(key, 37), BLOCKS - LONG_BLOCKS).astype(jnp.int32) + LONG_BLOCKS
    return jnp.concatenate([long_order, short_order]).astype(jnp.int32)


def block_scale(rng, dims, split, smallest, largest):
    factor_of = 1.0
    for axis_at, parts in split:
        heights = jax.random.uniform(jax.random.fold_in(jax.random.fold_in(rng, 6), axis_at), (parts,), jnp.float32, smallest / len(split), largest / len(split))
        factor_of = factor_of * jnp.repeat(jnp.exp(heights), dims[axis_at] // parts).reshape((-1,) + (1,) * (len(dims) - 1 - axis_at))
    return factor_of


def assign_block(key, own, number, rows, number_of, top, bound, skew):
    ranking = jax.random.permutation(key, number_of)
    heavy_load, usual = shares(number_of, rows * top, bound, skew, True), shares(number_of, rows * top, bound, skew, False)
    places = jnp.arange(number_of)

    def named(tallies, turn):
        used = int((tallies > 0).sum())
        fixed = max(1, used // 4)
        shifted = fixed + (places - fixed + turn * (used - fixed)) % max(1, number_of - fixed)
        return jnp.zeros((number_of,), jnp.int32).at[ranking[jnp.where(places < fixed, places, shifted)]].set(jnp.asarray(tallies, jnp.int32))

    tallies = jnp.where(number % 4 == 0, named(heavy_load, number // 4), named(usual, number - number // 4 - 1))
    mixed = jax.random.permutation(jax.random.fold_in(own, 3), number_of)
    source_of, receiver = mixed[0:number_of // 2 * 2:2], mixed[1:number_of // 2 * 2:2]
    room = jnp.minimum(tallies[source_of] - 1, bound - tallies[receiver]) // 2
    room = jnp.where((source_of == ranking[0]) | (receiver == ranking[0]) | (tallies[receiver] == 0), 0, jnp.maximum(room, 0))
    shifted = jax.random.randint(jax.random.fold_in(own, 4), (number_of // 2,), 0, 1 << 20) % (room + 1)
    tallies = tallies.at[source_of].add(-shifted).at[receiver].add(shifted)
    items = jnp.searchsorted(jnp.cumsum(tallies), jnp.arange(rows * top), side="right").astype(jnp.int32)
    listing = items.reshape(top, rows).T
    listing = listing[jax.random.permutation(jax.random.fold_in(own, 1), rows)]
    turn = jax.random.randint(jax.random.fold_in(own, 2), (rows, 1), 0, top)
    return jnp.take_along_axis(listing, (jnp.arange(top)[None, :] + turn) % top, axis=1)


def shares(number_of, total, reach, slope, full):
    weights = [(1 << 20) // math.isqrt(grade ** slope) + 1 for grade in range(1, number_of + 1)]
    largest = reach if full else min(reach, max(-(-total // number_of), total * weights[0] // sum(weights)))
    least = 1 if total - largest >= number_of - 1 else 0
    holding, rest = [largest] + [least] * (number_of - 1), total - largest - least * (number_of - 1)
    while rest > 0:
        movable = [i for i in range(1, number_of) if holding[i] < largest] or [i for i in range(1, number_of) if holding[i] < reach]
        pool, budget = sum([weights[i] for i in movable]), rest
        for i in movable:
            more = min(reach - holding[i], max(1, budget * weights[i] // pool), rest)
            holding[i] = holding[i] + more
            rest = rest - more
    return np.array(holding)


def gaussian(key, dims, deviation, most, pieces=(), held_as=jnp.bfloat16):
    loudness = block_scale(key, dims, pieces, -0.22, 0.18) if pieces else 1.0
    values = jax.random.normal(key, dims, jnp.float32) * deviation * loudness
    return jnp.minimum(jnp.maximum(values, -most), most).astype(held_as)


def setup_inputs(seed: int = 0) -> dict:
    splits = jax.random.split(jax.random.key(seed), 14)
    hidden = gaussian(splits[0], (PROMPT_TOKENS, D), 1.0, 6.0, ((0, 8), (1, 4)))
    queries = draw_queries(jax.random.fold_in(splits[13], 71), 0)
    keys = draw_keys(jax.random.fold_in(splits[13], 71), 0)
    values = gaussian(splits[3], (PROMPT_TOKENS, KEY_VALUE_HEADS * HEAD_SIZE), 1.0, 6.0, ((0, 8), (1, 4)))
    block_place = draw_block_place(jax.random.fold_in(splits[13], 71), 0)
    page_table = jax.random.permutation(splits[5], PAGE_TOTAL).astype(jnp.int32)
    out_weight = gaussian(splits[6], (QUERY_HEADS * HEAD_SIZE, D), (QUERY_HEADS * HEAD_SIZE) ** -0.5, 0.09375, ((0, 4),))
    norm_gain = jnp.clip(jnp.exp(jax.random.uniform(splits[7], (D,), jnp.float32, math.log(0.5), math.log(2.0))), 0.5, 2.0)
    gate_probs = jnp.clip(jnp.exp(math.log(1.0) - 2.3025851 * jax.random.uniform(splits[8], (PROMPT_TOKENS, TOP), jnp.float32) ** block_scale(splits[8], (PROMPT_TOKENS, TOP), ((0, 8),), -0.2, 0.2)), 0.1, 1.0)
    routes_keys = jax.random.split(jax.random.fold_in(splits[9], 1), PROMPT_TOKENS // TOKENS_PER_SEQ)
    routes_turns = jax.random.permutation(jax.random.fold_in(splits[9], 3), PROMPT_TOKENS // TOKENS_PER_SEQ)
    routes = jax.vmap(lambda own, number: assign_block(jax.random.fold_in(splits[9], 2), own, number, TOKENS_PER_SEQ, NEXP, TOP, CAP, 2))(routes_keys, routes_turns).reshape((PROMPT_TOKENS, TOP))
    w_gate = gaussian(splits[10], (NEXP, D, FF), D ** -0.5, 0.09375, ((0, 4), (2, 8)))
    w_up = gaussian(splits[11], (NEXP, D, FF), D ** -0.5, 0.09375, ((0, 4), (2, 8)))
    w_down = gaussian(splits[12], (NEXP, FF, D), FF ** -0.5, 0.046875, ((0, 4), (1, 8)))
    return dict(hidden=hidden, queries=queries, keys=keys, values=values, block_place=block_place, page_table=page_table, out_weight=out_weight, norm_gain=norm_gain, gate_probs=gate_probs, routes=routes, w_gate=w_gate, w_up=w_up, w_down=w_down)


THETA = 1000000.0
EPS = 1e-05

def apply_rotary(values_in, positions, head_count):
    row_count = values_in.shape[0]
    split_view = values_in.astype(jnp.float32).reshape(row_count, head_count, HEAD_SIZE)
    steps_half = jnp.arange(HEAD_SIZE // 2, dtype=jnp.float32)
    frequency = THETA ** (-(2.0 * steps_half) / HEAD_SIZE)
    angles = positions.astype(jnp.float32)[:, None] * frequency[None, :]
    cosine = jnp.cos(angles)[:, None, :]
    sine_part = jnp.sin(angles)[:, None, :]
    front_half = split_view[..., :HEAD_SIZE // 2]
    back_half = split_view[..., HEAD_SIZE // 2:]
    turned = jnp.concatenate([front_half * cosine - back_half * sine_part, back_half * cosine + front_half * sine_part], axis=-1)
    return turned.reshape(row_count, head_count * HEAD_SIZE).astype(jnp.bfloat16)

def expert_outputs(normed, routes, w_gate, w_up, w_down):
    assign_count = PROMPT_TOKENS * TOP
    flat_routes = routes.reshape(assign_count).astype(jnp.int32)
    order = jnp.argsort(flat_routes, stable=True).astype(jnp.int32)
    sorted_expert = flat_routes[order]
    sorted_rows = normed[order // TOP]
    block_rows = min(128, assign_count)

    def one_block(block_index):
        row_block = lax.dynamic_slice_in_dim(sorted_rows, block_index * block_rows, block_rows)
        expert_block = lax.dynamic_slice_in_dim(sorted_expert, block_index * block_rows, block_rows)

        def per_expert(expert_id, running):
            gate_part = jnp.dot(row_block, w_gate[expert_id], preferred_element_type=jnp.float32)
            up_part = jnp.dot(row_block, w_up[expert_id], preferred_element_type=jnp.float32)
            units = (jax.nn.silu(gate_part) * up_part).astype(jnp.bfloat16)
            result = jnp.dot(units, w_down[expert_id], preferred_element_type=jnp.float32)
            return jnp.where((expert_block == expert_id)[:, None], result, running)
        return lax.fori_loop(expert_block[0], expert_block[block_rows - 1] + 1, per_expert, jnp.zeros((block_rows, D), jnp.float32))
    outputs = lax.map(one_block, jnp.arange(assign_count // block_rows, dtype=jnp.int32))
    outputs = outputs.reshape(assign_count, D).astype(jnp.bfloat16)
    placed = jnp.zeros((assign_count, D), jnp.bfloat16).at[order].set(outputs)
    return placed.reshape(PROMPT_TOKENS, TOP, D)

def reference(hidden, queries, keys, values, block_place, page_table, out_weight, norm_gain, gate_probs, routes, w_gate, w_up, w_down):
    every_row = jnp.arange(PROMPT_TOKENS, dtype=jnp.int32)
    positions = (block_place[every_row // HALF] * HALF + every_row % HALF).astype(jnp.int32)
    in_long = positions >= LONG
    rotary_position = positions - LONG * in_long.astype(jnp.int32)
    query_rotated = apply_rotary(queries, rotary_position, QUERY_HEADS)
    key_rotated = apply_rotary(keys, rotary_position, KEY_VALUE_HEADS)
    row_at = jnp.argsort(positions).astype(jnp.int32)
    logical = jnp.argsort(page_table).astype(jnp.int32)
    page_token_rows = row_at[(logical[:, None] * PAGE_TOKENS + jnp.arange(PAGE_TOKENS, dtype=jnp.int32)[None, :]).reshape(PAGE_TOTAL * PAGE_TOKENS)]
    key_value_pages = jnp.stack([key_rotated[page_token_rows], values[page_token_rows]], axis=1).reshape(PAGE_TOTAL, PAGE_TOKENS, 2, KEY_VALUE_HEADS * HEAD_SIZE)
    query_head_group = QUERY_HEADS // KEY_VALUE_HEADS
    score_scale = 1.0 / math.sqrt(HEAD_SIZE)
    keys_expanded = key_rotated.astype(jnp.float32).reshape(PROMPT_TOKENS, KEY_VALUE_HEADS, HEAD_SIZE)
    values_expanded = values.astype(jnp.float32).reshape(PROMPT_TOKENS, KEY_VALUE_HEADS, HEAD_SIZE)

    def attend(block_index):
        leading_row = block_index * TOKENS_PER_SEQ
        query_tile_block = lax.dynamic_slice_in_dim(query_rotated, leading_row, TOKENS_PER_SEQ).astype(jnp.float32).reshape(TOKENS_PER_SEQ, KEY_VALUE_HEADS, query_head_group, HEAD_SIZE)
        query_pos = lax.dynamic_slice_in_dim(positions, leading_row, TOKENS_PER_SEQ)
        scores = jnp.einsum('tkgd,nkd->kgtn', query_tile_block, keys_expanded) * score_scale
        allowed = ((query_pos >= LONG)[:, None] == in_long[None, :]) & (positions[None, :] <= query_pos[:, None])
        scores = jnp.where(allowed, scores, -1e+30)
        row_peak = lax.optimization_barrier(jnp.max(scores, axis=-1, keepdims=True))
        weights = jnp.where(allowed, jnp.exp(scores - row_peak), 0.0)
        row_total = lax.optimization_barrier(jnp.sum(weights, axis=-1))
        rounded = lax.optimization_barrier(weights.astype(jnp.bfloat16)).astype(jnp.float32)
        mixed = jnp.einsum('kgtn,nkd->kgtd', rounded, values_expanded) / row_total[..., None]
        return mixed.transpose(2, 0, 1, 3).reshape(TOKENS_PER_SEQ, QUERY_HEADS * HEAD_SIZE).astype(jnp.bfloat16)
    attended = lax.map(attend, jnp.arange(PROMPT_TOKENS // TOKENS_PER_SEQ, dtype=jnp.int32)).reshape(PROMPT_TOKENS, QUERY_HEADS * HEAD_SIZE)
    projected = jnp.dot(attended, out_weight, preferred_element_type=jnp.float32)
    residual = (hidden.astype(jnp.float32) + projected).astype(jnp.bfloat16)
    residual_wide = residual.astype(jnp.float32)
    mean_square = lax.optimization_barrier(jnp.mean(residual_wide * residual_wide, axis=-1, keepdims=True))
    normed = (residual_wide * lax.rsqrt(mean_square + EPS) * norm_gain).astype(jnp.bfloat16)
    chosen = expert_outputs(normed, routes, w_gate, w_up, w_down).astype(jnp.float32)
    gate_share = gate_probs / lax.optimization_barrier(jnp.sum(gate_probs, axis=1, keepdims=True))
    layer_out = (residual_wide + lax.optimization_barrier(jnp.sum(gate_share[:, :, None] * chosen, axis=1))).astype(jnp.bfloat16)
    return (layer_out, key_value_pages)
```

```python
import math

import jax
import jax.numpy as jnp
from jax import lax
from jax.sharding import PartitionSpec as P

HEAD_SIZE = 128
NEXP = 8
PAGE_TOKENS = 16


THETA = 1000000.0
EPS = 1e-05


def apply_rotary(values_in, positions, head_count):
    row_count = values_in.shape[0]
    split_view = values_in.astype(jnp.float32).reshape(row_count, head_count, HEAD_SIZE)
    steps_half = jnp.arange(HEAD_SIZE // 2, dtype=jnp.float32)
    frequency = THETA ** (-(2.0 * steps_half) / HEAD_SIZE)
    angles = positions.astype(jnp.float32)[:, None] * frequency[None, :]
    cosine = jnp.cos(angles)[:, None, :]
    sine_part = jnp.sin(angles)[:, None, :]
    front_half = split_view[..., : HEAD_SIZE // 2]
    back_half = split_view[..., HEAD_SIZE // 2 :]
    turned = jnp.concatenate(
        [front_half * cosine - back_half * sine_part, back_half * cosine + front_half * sine_part],
        axis=-1,
    )
    return turned.reshape(row_count, head_count * HEAD_SIZE).astype(jnp.bfloat16)


def per_device(
    hidden,
    queries,
    keys,
    values,
    block_place,
    page_table,
    out_weight,
    norm_gain,
    gate_probs,
    routes,
    w_gate,
    w_up,
    w_down,
):
    seq_count = lax.axis_size("seq")
    exp_count = lax.axis_size("exp")
    seq_index = lax.axis_index("seq")
    exp_index = lax.axis_index("exp")
    tok_rows = queries.shape[0]
    half_rows = tok_rows // 2
    all_rows = tok_rows * seq_count
    long_len = 3 * all_rows // 4
    blocks = block_place.shape[0]
    within = jnp.arange(half_rows, dtype=jnp.int32)
    all_pos = (block_place[:, None] * half_rows + within[None, :]).reshape(all_rows)
    my_blocks = lax.dynamic_slice_in_dim(block_place, seq_index * 2, 2)
    my_pos = (my_blocks[:, None] * half_rows + within[None, :]).reshape(tok_rows)
    my_long = my_pos >= long_len
    my_rope = my_pos - long_len * my_long.astype(jnp.int32)
    q_heads = queries.shape[1] // HEAD_SIZE
    kv_heads = keys.shape[1] // HEAD_SIZE
    kv_width = keys.shape[1]
    group = q_heads // kv_heads
    key_rotated = apply_rotary(keys, my_rope, kv_heads)
    kv_all = lax.all_gather(
        jnp.concatenate([key_rotated, values], axis=1), "seq", axis=0, tiled=True
    )
    query_rotated = apply_rotary(queries, my_rope, q_heads)
    q_grid = query_rotated.reshape(tok_rows, kv_heads, group, HEAD_SIZE)
    key_all = kv_all[:, :kv_width].reshape(all_rows, kv_heads, HEAD_SIZE)
    value_all = kv_all[:, kv_width:].reshape(all_rows, kv_heads, HEAD_SIZE)
    scores = jnp.einsum(
        "tkgd,nkd->kgtn", q_grid, key_all, preferred_element_type=jnp.float32
    ) * (1.0 / math.sqrt(HEAD_SIZE))
    allowed = ((all_pos >= long_len)[None, :] == my_long[:, None]) & (
        all_pos[None, :] <= my_pos[:, None]
    )
    scores = jnp.where(allowed, scores, -1e30)
    peak = jnp.max(scores, axis=-1)
    weights = jnp.where(allowed, jnp.exp(scores - peak[..., None]), 0.0)
    total = jnp.sum(weights, axis=-1)
    summed = jnp.einsum(
        "kgtn,nkd->kgtd",
        weights.astype(jnp.bfloat16),
        value_all,
        preferred_element_type=jnp.float32,
    )
    attended = (
        (summed / total[..., None])
        .transpose(2, 0, 1, 3)
        .reshape(tok_rows, q_heads * HEAD_SIZE)
        .astype(jnp.bfloat16)
    )
    partial_proj = jnp.dot(attended, out_weight, preferred_element_type=jnp.float32)
    projected = lax.psum_scatter(
        partial_proj.astype(jnp.bfloat16), "exp", scatter_dimension=1, tiled=True
    ).astype(jnp.float32)
    residual = (hidden.astype(jnp.float32) + projected).astype(jnp.bfloat16)

    page_count = tok_rows // PAGE_TOKENS
    page_total = page_table.shape[0]
    per_block = half_rows // PAGE_TOKENS
    my_pages = seq_index * page_count + jnp.arange(page_count, dtype=jnp.int32)
    logical = jnp.sum(
        jnp.where(
            page_table[None, :] == my_pages[:, None],
            jnp.arange(page_total, dtype=jnp.int32)[None, :],
            0,
        ),
        axis=1,
    )
    holder = jnp.sum(
        jnp.where(
            block_place[None, :] == (logical // per_block)[:, None],
            jnp.arange(blocks, dtype=jnp.int32)[None, :],
            0,
        ),
        axis=1,
    )
    source_page = holder * per_block + logical % per_block
    kv_pages = kv_all.reshape(page_total, PAGE_TOKENS, 2 * kv_width)
    cache_pages = jnp.concatenate(
        [lax.dynamic_slice_in_dim(kv_pages, source_page[i], 1) for i in range(page_count)]
    ).reshape(page_count, PAGE_TOKENS, 2, kv_width)

    expert_local = NEXP // exp_count
    capacity = tok_rows // 2
    my_experts = exp_index * expert_local + jnp.arange(expert_local, dtype=jnp.int32)
    hot = routes[:, None, :] == my_experts[None, :, None]
    hit = jnp.any(hot, axis=-1)
    earlier = (jnp.arange(tok_rows)[:, None] > jnp.arange(tok_rows)[None, :]).astype(jnp.bfloat16)
    rank = jnp.dot(
        earlier, hit.astype(jnp.bfloat16), preferred_element_type=jnp.float32
    ).astype(jnp.int32)
    slot_of = jnp.where(hit, rank, -1).T
    chooser = (
        slot_of[:, None, :] == jnp.arange(capacity, dtype=jnp.int32)[None, :, None]
    ).astype(jnp.bfloat16)
    gate_share = gate_probs / jnp.sum(gate_probs, axis=1, keepdims=True)
    share = jnp.sum(jnp.where(hot, gate_share[:, None, :], 0.0), axis=-1)

    residual_full = lax.all_gather(residual, "exp", axis=1, tiled=True).astype(jnp.float32)
    mean_square = jnp.mean(residual_full * residual_full, axis=-1, keepdims=True)
    normed = (residual_full * lax.rsqrt(mean_square + EPS) * norm_gain).astype(jnp.bfloat16)
    token_rows = [
        lax.all_gather(
            jnp.dot(chooser[j], normed, preferred_element_type=jnp.float32).astype(jnp.bfloat16),
            "seq",
            axis=0,
            tiled=True,
        )
        for j in range(expert_local)
    ]
    mixed = 0.0
    for j in range(expert_local):
        gate_part = jnp.dot(token_rows[j], w_gate[j], preferred_element_type=jnp.float32)
        up_part = jnp.dot(token_rows[j], w_up[j], preferred_element_type=jnp.float32)
        units = (jax.nn.silu(gate_part) * up_part).astype(jnp.bfloat16)
        returned = lax.psum_scatter(
            jnp.dot(units, w_down[j], preferred_element_type=jnp.float32).astype(jnp.bfloat16),
            "seq",
            scatter_dimension=0,
            tiled=True,
        )
        placed = lax.dot_general(
            chooser[j], returned, (((0,), (0,)), ((), ())), preferred_element_type=jnp.float32
        )
        mixed = mixed + share[:, j : j + 1] * placed
    chosen = lax.psum_scatter(mixed.astype(jnp.bfloat16), "exp", scatter_dimension=1, tiled=True)
    layer_out = (residual.astype(jnp.float32) + chosen.astype(jnp.float32)).astype(jnp.bfloat16)
    return (layer_out, cache_pages)


def solution(mesh):
    return jax.shard_map(
        per_device,
        mesh=mesh,
        in_specs=(
            P("seq", "exp"),
            P("seq", "exp"),
            P("seq", "exp"),
            P("seq", "exp"),
            P(),
            P(),
            P("exp", None),
            P(),
            P("seq", None),
            P("seq", None),
            P("exp", None, "seq"),
            P("exp", None, "seq"),
            P("exp", "seq", None),
        ),
        out_specs=(P("seq", "exp"), P("seq", None, None, "exp")),
        check_vma=False,
    )
```

```python
import functools
import math

import jax
import jax.numpy as jnp
from jax import lax
from jax.experimental import pallas as pl
from jax.experimental.pallas import tpu as pltpu
from jax.sharding import PartitionSpec as P

HEAD_SIZE = 128
NEXP = 8
PAGE_TOKENS = 16


THETA = 1000000.0
EPS = 1e-05


def apply_rotary(values_in, positions, head_count):
    row_count = values_in.shape[0]
    split_view = values_in.astype(jnp.float32).reshape(row_count, head_count, HEAD_SIZE)
    steps_half = jnp.arange(HEAD_SIZE // 2, dtype=jnp.float32)
    frequency = THETA ** (-(2.0 * steps_half) / HEAD_SIZE)
    angles = positions.astype(jnp.float32)[:, None] * frequency[None, :]
    cosine = jnp.cos(angles)[:, None, :]
    sine_part = jnp.sin(angles)[:, None, :]
    front_half = split_view[..., : HEAD_SIZE // 2]
    back_half = split_view[..., HEAD_SIZE // 2 :]
    turned = jnp.concatenate(
        [front_half * cosine - back_half * sine_part, back_half * cosine + front_half * sine_part],
        axis=-1,
    )
    return turned.reshape(row_count, head_count * HEAD_SIZE).astype(jnp.bfloat16)


MESH = pl.DeviceIdType.MESH


def divisor_tile(size, choices):
    for choice in choices:
        if size % choice == 0:
            return choice
    return size


def experts_kernel(
    n, x_ref, wg_ref, wu_ref, wd_ref, out_ref,
    rows, units, part, inbox, gs, gr, rs, rr,
):
    experts, cap, width = x_ref.shape
    inner = wg_ref.shape[2]
    total_rows = n * cap
    step_rows = 256
    me = lax.axis_index("seq")
    exp_me = lax.axis_index("exp")

    def peer(k):
        return (lax.rem(me + k, n), exp_me)

    def rows_of(index):
        return pl.ds(pl.multiple_of(index * cap, cap), cap)

    barrier = pltpu.get_barrier_semaphore()
    for k in range(1, n):
        pl.semaphore_signal(barrier, inc=1, device_id=peer(k), device_id_type=MESH)
    pl.semaphore_wait(barrier, n - 1)

    def gather_copy(e, k):
        return pltpu.make_async_remote_copy(
            src_ref=x_ref.at[e],
            dst_ref=rows.at[e, rows_of(me)],
            send_sem=gs.at[e, k - 1],
            recv_sem=gr.at[e, k - 1],
            device_id=peer(k),
            device_id_type=MESH,
        )

    def return_copy(e, h, k):
        half = width // 2
        columns = pl.ds(h * half, half)
        return pltpu.make_async_remote_copy(
            src_ref=part.at[e, rows_of(lax.rem(me + k, n)), columns],
            dst_ref=inbox.at[e, rows_of(me), columns],
            send_sem=rs.at[e, h, k - 1],
            recv_sem=rr.at[e, h, k - 1],
            device_id=peer(k),
            device_id_type=MESH,
        )

    gate_tile = divisor_tile(inner, (256, 128))
    down_tile = 512

    def start_gather(e):
        for k in range(1, n):
            gather_copy(e, k).start()
        rows[e, rows_of(me)] = x_ref[e]

    def end_gather(e):
        for k in range(1, n):
            gather_copy(e, k).wait_recv()

    start_gather(0)
    for e in range(experts):
        end_gather(e)
        if e + 1 < experts:
            start_gather(e + 1)

        def gate_body(wg_tile, wu_tile, e=e):
            column = pl.multiple_of(pl.program_id(0) * gate_tile, gate_tile)

            @pl.loop(0, total_rows // step_rows)
            def _(m):
                at = pl.ds(pl.multiple_of(m * step_rows, step_rows), step_rows)
                x = rows[e, at]
                gate = jnp.dot(x, wg_tile[...], preferred_element_type=jnp.float32)
                up = jnp.dot(x, wu_tile[...], preferred_element_type=jnp.float32)
                units[at, pl.ds(column, gate_tile)] = (
                    gate / (1.0 + jnp.exp(-gate)) * up
                ).astype(jnp.bfloat16)

        spec = pl.BlockSpec((width, gate_tile), lambda j: (0, j))
        pltpu.emit_pipeline(
            gate_body,
            grid=(inner // gate_tile,),
            in_specs=[spec, spec],
            out_specs=[],
        )(wg_ref.at[e], wu_ref.at[e])

        for h in range(2):

            def down_body(wd_tile, e=e, h=h):
                column = pl.multiple_of(h * (width // 2) + pl.program_id(0) * down_tile, down_tile)

                @pl.loop(0, total_rows // step_rows)
                def _(m):
                    at = pl.ds(pl.multiple_of(m * step_rows, step_rows), step_rows)
                    part[e, at, pl.ds(column, down_tile)] = jnp.dot(
                        units[at], wd_tile[...], preferred_element_type=jnp.float32
                    ).astype(jnp.bfloat16)

            per_half = width // 2 // down_tile
            pltpu.emit_pipeline(
                down_body,
                grid=(per_half,),
                in_specs=[
                    pl.BlockSpec((inner, down_tile), lambda j, h=h: (0, h * per_half + j))
                ],
                out_specs=[],
            )(wd_ref.at[e])
            for k in range(1, n):
                return_copy(e, h, k).start()

    for e in range(experts):
        for h in range(2):
            for k in range(1, n):
                return_copy(e, h, k).wait_recv()
        piece = 16

        @pl.loop(0, cap // piece)
        def _(r):
            at = pl.multiple_of(r * piece, piece)
            total = part[e, pl.ds(pl.multiple_of(me * cap + at, piece), piece)].astype(jnp.float32)
            for k in range(1, n):
                sender = lax.rem(me + n - k, n)
                total += inbox[
                    e, pl.ds(pl.multiple_of(sender * cap + at, piece), piece)
                ].astype(jnp.float32)
            out_ref[e, pl.ds(at, piece)] = total.astype(jnp.bfloat16)

    for e in range(experts):
        for k in range(1, n):
            gather_copy(e, k).wait_send()
            for h in range(2):
                return_copy(e, h, k).wait_send()


def run_experts(n, x, w_gate, w_up, w_down):
    experts, cap, width = x.shape
    inner = w_gate.shape[2]
    vmem = pl.BlockSpec(memory_space=pltpu.VMEM)
    anywhere = pl.BlockSpec(memory_space=pl.ANY)
    big = pltpu.VMEM((experts, n * cap, width), jnp.bfloat16)
    return pl.pallas_call(
        functools.partial(experts_kernel, n),
        out_shape=jax.ShapeDtypeStruct(x.shape, jnp.bfloat16),
        in_specs=[vmem, anywhere, anywhere, anywhere],
        out_specs=vmem,
        scratch_shapes=[
            big,
            pltpu.VMEM((n * cap, inner), jnp.bfloat16),
            big,
            big,
            pltpu.SemaphoreType.DMA((experts, n - 1)),
            pltpu.SemaphoreType.DMA((experts, n - 1)),
            pltpu.SemaphoreType.DMA((experts, 2, n - 1)),
            pltpu.SemaphoreType.DMA((experts, 2, n - 1)),
        ],
        compiler_params=pltpu.CompilerParams(
            collective_id=0, has_side_effects=True, vmem_limit_bytes=56 * 1024 * 1024
        ),
        cost_estimate=pl.CostEstimate(
            flops=6 * experts * n * cap * width * inner,
            bytes_accessed=6 * experts * width * inner,
            transcendentals=experts * n * cap * inner,
        ),
    )(x, w_gate, w_up, w_down)


def per_device(
    hidden,
    queries,
    keys,
    values,
    block_place,
    page_table,
    out_weight,
    norm_gain,
    gate_probs,
    routes,
    w_gate,
    w_up,
    w_down,
):
    seq_count = lax.axis_size("seq")
    exp_count = lax.axis_size("exp")
    seq_index = lax.axis_index("seq")
    exp_index = lax.axis_index("exp")
    tok_rows = queries.shape[0]
    half_rows = tok_rows // 2
    all_rows = tok_rows * seq_count
    long_len = 3 * all_rows // 4
    blocks = block_place.shape[0]
    within = jnp.arange(half_rows, dtype=jnp.int32)
    all_pos = (block_place[:, None] * half_rows + within[None, :]).reshape(all_rows)
    my_blocks = lax.dynamic_slice_in_dim(block_place, seq_index * 2, 2)
    my_pos = (my_blocks[:, None] * half_rows + within[None, :]).reshape(tok_rows)
    my_long = my_pos >= long_len
    my_rope = my_pos - long_len * my_long.astype(jnp.int32)
    q_heads = queries.shape[1] // HEAD_SIZE
    kv_heads = keys.shape[1] // HEAD_SIZE
    kv_width = keys.shape[1]
    group = q_heads // kv_heads
    key_rotated = apply_rotary(keys, my_rope, kv_heads)
    kv_all = lax.all_gather(
        jnp.concatenate([key_rotated, values], axis=1), "seq", axis=0, tiled=True
    )
    query_rotated = apply_rotary(queries, my_rope, q_heads)
    q_grid = query_rotated.reshape(tok_rows, kv_heads, group, HEAD_SIZE)
    key_all = kv_all[:, :kv_width].reshape(all_rows, kv_heads, HEAD_SIZE)
    value_all = kv_all[:, kv_width:].reshape(all_rows, kv_heads, HEAD_SIZE)
    scores = jnp.einsum(
        "tkgd,nkd->kgtn", q_grid, key_all, preferred_element_type=jnp.float32
    ) * (1.0 / math.sqrt(HEAD_SIZE))
    allowed = ((all_pos >= long_len)[None, :] == my_long[:, None]) & (
        all_pos[None, :] <= my_pos[:, None]
    )
    scores = jnp.where(allowed, scores, -1e30)
    peak = jnp.max(scores, axis=-1)
    weights = jnp.where(allowed, jnp.exp(scores - peak[..., None]), 0.0)
    total = jnp.sum(weights, axis=-1)
    summed = jnp.einsum(
        "kgtn,nkd->kgtd",
        weights.astype(jnp.bfloat16),
        value_all,
        preferred_element_type=jnp.float32,
    )
    attended = (
        (summed / total[..., None])
        .transpose(2, 0, 1, 3)
        .reshape(tok_rows, q_heads * HEAD_SIZE)
        .astype(jnp.bfloat16)
    )
    partial_proj = jnp.dot(attended, out_weight, preferred_element_type=jnp.float32)
    projected = lax.psum_scatter(
        partial_proj.astype(jnp.bfloat16), "exp", scatter_dimension=1, tiled=True
    ).astype(jnp.float32)
    residual = (hidden.astype(jnp.float32) + projected).astype(jnp.bfloat16)

    page_count = tok_rows // PAGE_TOKENS
    page_total = page_table.shape[0]
    per_block = half_rows // PAGE_TOKENS
    my_pages = seq_index * page_count + jnp.arange(page_count, dtype=jnp.int32)
    logical = jnp.sum(
        jnp.where(
            page_table[None, :] == my_pages[:, None],
            jnp.arange(page_total, dtype=jnp.int32)[None, :],
            0,
        ),
        axis=1,
    )
    holder = jnp.sum(
        jnp.where(
            block_place[None, :] == (logical // per_block)[:, None],
            jnp.arange(blocks, dtype=jnp.int32)[None, :],
            0,
        ),
        axis=1,
    )
    source_page = holder * per_block + logical % per_block
    kv_pages = kv_all.reshape(page_total, PAGE_TOKENS, 2 * kv_width)
    cache_pages = jnp.concatenate(
        [lax.dynamic_slice_in_dim(kv_pages, source_page[i], 1) for i in range(page_count)]
    ).reshape(page_count, PAGE_TOKENS, 2, kv_width)

    expert_local = NEXP // exp_count
    capacity = tok_rows // 2
    my_experts = exp_index * expert_local + jnp.arange(expert_local, dtype=jnp.int32)
    hot = routes[:, None, :] == my_experts[None, :, None]
    hit = jnp.any(hot, axis=-1)
    earlier = (jnp.arange(tok_rows)[:, None] > jnp.arange(tok_rows)[None, :]).astype(jnp.bfloat16)
    rank = jnp.dot(
        earlier, hit.astype(jnp.bfloat16), preferred_element_type=jnp.float32
    ).astype(jnp.int32)
    slot_of = jnp.where(hit, rank, -1).T
    chooser = (
        slot_of[:, None, :] == jnp.arange(capacity, dtype=jnp.int32)[None, :, None]
    ).astype(jnp.bfloat16)
    gate_share = gate_probs / jnp.sum(gate_probs, axis=1, keepdims=True)
    share = jnp.sum(jnp.where(hot, gate_share[:, None, :], 0.0), axis=-1)

    residual_full = lax.all_gather(residual, "exp", axis=1, tiled=True).astype(jnp.float32)
    mean_square = jnp.mean(residual_full * residual_full, axis=-1, keepdims=True)
    normed = (residual_full * lax.rsqrt(mean_square + EPS) * norm_gain).astype(jnp.bfloat16)
    slots = jnp.einsum(
        "est,td->esd", chooser, normed, preferred_element_type=jnp.float32
    ).astype(jnp.bfloat16)
    returned = run_experts(seq_count, slots, w_gate, w_up, w_down)
    mixed = 0.0
    for j in range(expert_local):
        placed = lax.dot_general(
            chooser[j], returned[j], (((0,), (0,)), ((), ())), preferred_element_type=jnp.float32
        )
        mixed = mixed + share[:, j : j + 1] * placed
    chosen = lax.psum_scatter(mixed.astype(jnp.bfloat16), "exp", scatter_dimension=1, tiled=True)
    layer_out = (residual.astype(jnp.float32) + chosen.astype(jnp.float32)).astype(jnp.bfloat16)
    return (layer_out, cache_pages)


def solution(mesh):
    return jax.shard_map(
        per_device,
        mesh=mesh,
        in_specs=(
            P("seq", "exp"),
            P("seq", "exp"),
            P("seq", "exp"),
            P("seq", "exp"),
            P(),
            P(),
            P("exp", None),
            P(),
            P("seq", None),
            P("seq", None),
            P("exp", None, "seq"),
            P("exp", None, "seq"),
            P("exp", "seq", None),
        ),
        out_specs=(P("seq", "exp"), P("seq", None, None, "exp")),
        check_vma=False,
    )
```
